512 devices in a mesh: head: 8 (over z_hi, core), blk: 64 (over z_lo, x, y).
Axes of the slice: x: 4, y: 4, z: 16 (z_hi: 4, z_lo: 4; z = z_hi * 4 + z_lo), core: 2. Of those that a mesh axis runs over, the one named last changes fastest.
Arguments:
- queries: bfloat16 [8192, 3072], P(('blk', 'head'))
- keys_in: bfloat16 [8192, 3072], P(('blk', 'head'))
- values: bfloat16 [8192, 3072], P(('blk', 'head')), may hold values from -6 to 6
- block_mask: int32 [24, 64, 64], P('head', 'blk'), may hold values from 0 to 1, as said below
- w_out: bfloat16 [3072, 3072], P('head'), may hold values from -0.109375 to 0.109375
Outputs:
- mixed: bfloat16 [8192, 3072], P(('blk', 'head'))
The draws below stay inside these ranges and needn't reach their ends.
Inputs may be any that keep to these rules, and one draw needn't show every extreme that they name: block_mask[h, i, i] = 1, block_mask[h, i, i - 1] = 1 and block_mask[h, i, i + 1] = 1 where those blocks exist, and block_mask[h, i, 0] = 1, for every head and query block; elsewhere the share of ones falls with the distance |i - j| and differs from head to head and from query block to query block.
All inputs are finite; a program needn't handle non-finite values.
Results may differ from the reference program's by a relative error of at most 0.02.
Values may be sent and summed in bfloat16 or wider, within the bound.
No kernel may reach another device: no remote copies, remote signals or barrier semaphores. Data moves between devices by JAX's collectives and lax.ppermute only.
A program may use at most 128 MiB of HBM per device.

```python
import jax
import jax.numpy as jnp
from jax import lax

H = 24
DH = 128
D = 3072
BLOCK = 128
NB = 64
TOKENS = 8192


def shared_keys(key):
    return jnp.clip(jax.random.normal(key, (TOKENS, D), jnp.float32), -6.0, 6.0)


def draw_keys_in(key, part):
    base = shared_keys(key)
    return base.astype(jnp.bfloat16)


def draw_queries(key, part):
    key = jax.random.fold_in(key, 5)
    own = jnp.clip(jax.random.normal(key, (TOKENS, D), jnp.float32), -6.0, 6.0)
    return own.astype(jnp.bfloat16)


def draw_block_mask(key, part):
    key = jax.random.fold_in(key, 11)
    first_key, second_key, third_key = jax.random.split(key, 3)
    rates = jax.random.randint(first_key, (H, 1, 1), 1, 9)
    factors = jax.random.randint(third_key, (1, NB, 1), 1, 5)
    chances = jax.random.randint(second_key, (H, NB, NB), 0, 1024)
    index_row = jnp.arange(NB, dtype=jnp.int32)
    distance = jnp.abs(index_row[:, None] - index_row[None, :])[None, :, :]
    sink_column = index_row[None, None, :] == 0
    kept = (distance <= 1) | sink_column | (chances * distance < 48 * rates * factors)
    return kept.astype(jnp.int32)


def levels(stream_key, extent, shards, smallest, top_value):
    def one(position, parts):
        heights = jax.random.uniform(jax.random.fold_in(jax.random.fold_in(stream_key, 6), position), (parts,), jnp.float32, smallest / len(shards), top_value / len(shards))
        return jnp.repeat(jnp.exp(heights), extent[position] // parts).reshape((-1,) + (1,) * (len(extent) - position - 1))

    gain = one(*shards[0])
    for cut in shards[1:]:
        gain = gain * one(*cut)
    return gain


def noise(stream_key, extent, deviation, limit, shards=(), kind=jnp.bfloat16):
    entries = deviation * jax.random.normal(stream_key, extent, jnp.float32)
    if shards:
        entries = entries * levels(stream_key, extent, shards, -0.22, 0.18)
    return jnp.clip(entries, -limit, limit).astype(kind)


def setup_inputs(seed: int = 0) -> dict:
    splits = jax.random.split(jax.random.key(seed), 6)
    return {
        "queries": draw_queries(jax.random.fold_in(splits[5], 71), 0),
        "keys_in": draw_keys_in(jax.random.fold_in(splits[5], 71), 0),
        "values": noise(splits[2], (TOKENS, D), 1.0, 6.0, ((0, 512),)),
        "block_mask": draw_block_mask(jax.random.fold_in(splits[5], 71), 0),
        "w_out": noise(splits[4], (D, D), D ** -0.5, 0.109375, ((0, 8),)),
    }


def reference(queries, keys_in, values, block_mask, w_out):
    inv_root = 1.0 / (DH ** 0.5)

    def attend_block(flat_index):
        head_at = flat_index // NB
        block_at = flat_index % NB
        query_rows = lax.dynamic_slice(queries, ((block_at * BLOCK).astype(jnp.int32), (head_at * DH).astype(jnp.int32)), (BLOCK, DH))
        key_cols = lax.dynamic_slice_in_dim(keys_in, (head_at * DH).astype(jnp.int32), DH, 1)
        value_cols = lax.dynamic_slice_in_dim(values, (head_at * DH).astype(jnp.int32), DH, 1)
        kept_keys = jnp.repeat(block_mask[head_at, block_at], BLOCK) > 0
        scores = jnp.dot(query_rows, key_cols.T, preferred_element_type=jnp.float32) * inv_root
        largest = jnp.max(jnp.where(kept_keys[None, :], scores, -jnp.inf), axis=1)
        weights = jnp.where(kept_keys[None, :], jnp.exp(scores - largest[:, None]), 0.0)
        total = jnp.sum(weights, axis=1)
        rounded_weights = weights.astype(jnp.bfloat16)
        summed = jnp.dot(rounded_weights, value_cols, preferred_element_type=jnp.float32)
        return (summed / total[:, None]).astype(jnp.bfloat16)

    pieces = lax.map(attend_block, jnp.arange(H * NB, dtype=jnp.int32))
    attended = pieces.reshape(H, TOKENS, DH).transpose(1, 0, 2).reshape(TOKENS, H * DH)
    return jnp.dot(attended, w_out, preferred_element_type=jnp.float32).astype(jnp.bfloat16)
```

```python
import functools

import jax
import jax.numpy as jnp
from jax import lax
from jax.experimental import pallas as pl
from jax.experimental.pallas import tpu as pltpu
from jax.sharding import Mesh, PartitionSpec as P

BF = jnp.bfloat16
F32 = jnp.float32
AXES = ("z_hi", "core", "z_lo", "x", "y")
LOW = -1e30
LOG2E = 1.4426950408889634


def pack_kernel(q_ref, k_ref, v_ref, mask_ref, out_ref):
    seen = jnp.concatenate([mask_ref[...].astype(F32), jnp.zeros((3, 64), F32)], axis=1)
    for slot in range(4):
        row = seen[min(slot, 2) : min(slot, 2) + 1]
        tail = jnp.concatenate([row, jnp.zeros((7, 128), F32)], axis=0).astype(BF)
        for core in range(2):
            for z_hi in range(4):
                head = 3 * (2 * z_hi + core) + slot
                place = slot * 8 + core * 4 + z_hi
                for part, ref in enumerate((q_ref, k_ref, v_ref)):
                    rows = slice(part * 16, part * 16 + 16)
                    if slot < 3:
                        out_ref[place, rows, :] = ref[:, head * 128 : head * 128 + 128]
                    else:
                        out_ref[place, rows, :] = jnp.zeros((16, 128), BF)
                out_ref[place, 48:56, :] = tail


def pack(queries, keys, values, mask):
    return pl.pallas_call(
        pack_kernel,
        out_shape=jax.ShapeDtypeStruct((32, 56, 128), BF),
        name="pack",
    )(queries, keys, values, mask)


def spread_kernel(at_ref, in_ref, q_ref, kv_ref):
    mine = at_ref[4] * 4 + at_ref[3]
    for place in range(32):
        rows = slice(place * 16, place * 16 + 16)
        q_ref[rows, :] = in_ref[place, 0:16, :]
        for there in range(4):
            kv_ref[there, rows, 0:128] = in_ref[place, 16:32, :]
            kv_ref[there, rows, 128:256] = in_ref[place, 32:48, :]
    tails = [in_ref[z * 8 + mine, 48:56, :].astype(F32)[0:1] for z in range(4)]
    q_ref[512:528, :] = jnp.concatenate(tails + [jnp.zeros((12, 128), F32)], axis=0).astype(BF)


def spread(at, mine):
    return pl.pallas_call(
        spread_kernel,
        out_shape=[
            jax.ShapeDtypeStruct((528, 128), BF),
            jax.ShapeDtypeStruct((4, 512, 256), BF),
        ],
        in_specs=[
            pl.BlockSpec(memory_space=pltpu.SMEM),
            pl.BlockSpec(memory_space=pltpu.VMEM),
        ],
        name="spread",
    )(at, mine)


def attend_kernel(
    at_ref, q0, q1, q2, q3, kv_ref, out_ref, vt_ref, rows_ref, list_ref, mask_ref, sem
):
    x = at_ref[0]
    qs = (q0, q1, q2, q3)
    scale = LOG2E / 128**0.5
    for dq in range(4):
        rows_ref[dq * 8 : dq * 8 + 8, :] = qs[dq][512:528, :].astype(F32)[0:8].astype(jnp.int32)
    to_scalars = pltpu.make_async_copy(rows_ref, mask_ref, sem)
    to_scalars.start()
    for block in range(16):
        vt_ref[block] = kv_ref[block, :, 128:].T
    to_scalars.wait()

    for dq in range(4):
        xq = (x + 4 - dq) % 4
        counts = []
        for zq in range(4):
            count = jnp.int32(0)
            for block in range(16):
                list_ref[zq, count] = block
                seen = mask_ref[dq * 8 + zq, (block % 4) * 16 + 4 * x + block // 4]
                count = count + jnp.where(seen > 0, 1, 0)
            counts.append(count)
        most = jnp.maximum(jnp.maximum(counts[0], counts[1]), jnp.maximum(counts[2], counts[3]))
        queries = [qs[dq][zq * 128 : zq * 128 + 128, :] for zq in range(4)]

        def fold(step, states, queries=queries, counts=counts):
            after = []
            for zq in range(4):
                largest, total, acc = states[zq]
                blocks, pieces = [], []
                for part in range(4):
                    place = step * 4 + part
                    here = place < counts[zq]
                    block = jnp.where(here, list_ref[zq, jnp.where(here, place, 0)], 0)
                    piece = lax.dot_general(
                        kv_ref[block, :, :128],
                        queries[zq],
                        (((1,), (1,)), ((), ())),
                        preferred_element_type=F32,
                    )
                    pieces.append(piece * scale + jnp.where(here, 0.0, LOW))
                    blocks.append(block)
                scores = jnp.concatenate(pieces, axis=0)
                new = jnp.maximum(largest, jnp.max(scores, axis=0, keepdims=True))
                weights = jnp.exp2(scores - new)
                again = jnp.exp2(largest - new)
                total = total * again + jnp.sum(weights, axis=0, keepdims=True)
                turned = jnp.concatenate([vt_ref[block] for block in blocks], axis=1)
                product = jnp.dot(turned, weights.astype(BF), preferred_element_type=F32)
                after.append((new, total, acc * again + product))
            return tuple(after)

        start = (
            jnp.full((1, 128), LOW, F32),
            jnp.zeros((1, 128), F32),
            jnp.zeros((128, 128), F32),
        )
        states = lax.fori_loop(0, (most + 3) // 4, fold, (start,) * 4)
        for zq in range(4):
            largest, total, acc = states[zq]
            empty = total == 0.0
            inverse = jnp.where(empty, 0.0, 1.0 / jnp.where(empty, 1.0, total))
            o = (acc * inverse).T.astype(BF)
            lse = largest + jnp.log2(jnp.where(empty, 1.0, total))
            hi = lse.astype(BF)
            rest = lse - hi.astype(F32)
            mid = rest.astype(BF)
            lo = (rest - mid.astype(F32)).astype(BF)
            coded = jnp.concatenate(
                [hi.astype(F32), mid.astype(F32), lo.astype(F32), jnp.zeros((13, 128), F32)], axis=0
            )
            turned = jnp.concatenate([coded[:, 64:], coded[:, :64]], axis=1)
            place = (xq * 4 + zq) * 2
            out_ref[place, 0:64, :] = o[0:64]
            out_ref[place, 64:80, :] = coded.astype(BF)
            out_ref[place + 1, 0:64, :] = o[64:128]
            out_ref[place + 1, 64:80, :] = turned.astype(BF)


def attend(at, qs, kv):
    smem = pl.BlockSpec(memory_space=pltpu.SMEM)
    vmem = pl.BlockSpec(memory_space=pltpu.VMEM)
    return pl.pallas_call(
        attend_kernel,
        out_shape=jax.ShapeDtypeStruct((32, 80, 128), BF),
        in_specs=[smem] + [vmem] * 5,
        out_specs=vmem,
        scratch_shapes=[
            pltpu.VMEM((16, 128, 128), BF),
            pltpu.VMEM((32, 128), jnp.int32),
            pltpu.SMEM((4, 17), jnp.int32),
            pltpu.SMEM((32, 128), jnp.int32),
            pltpu.SemaphoreType.DMA,
        ],
        compiler_params=pltpu.CompilerParams(vmem_limit_bytes=48 * 1024 * 1024),
        cost_estimate=pl.CostEstimate(flops=1 << 30, bytes_accessed=2 << 20, transcendentals=1 << 21),
        name="attend",
    )(at, *qs, kv)


def project_kernel(at_ref, parts_ref, own_ref, other_ref, y0, y1, y2, y3, att_ref):
    z_hi, core = at_ref[3], at_ref[4]

    @pl.when(pl.program_id(0) == 0)
    def _():
        coded = [parts_ref[i, 64:80, :].astype(F32) for i in range(32)]
        lse = jnp.concatenate([c[0:1] + c[1:2] + c[2:3] for c in coded], axis=0)
        groups = [lse[8 * i : 8 * i + 8] for i in range(4)]
        top = jnp.maximum(jnp.maximum(groups[0], groups[1]), jnp.maximum(groups[2], groups[3]))
        shares = [jnp.exp2(g - top) for g in groups]
        total = shares[0] + shares[1] + shares[2] + shares[3]
        inverse = 1.0 / total
        share = jnp.concatenate([s * inverse for s in shares], axis=0)
        share = jnp.concatenate([share, jnp.zeros((96, 128), F32)], axis=0).T
        for slot in range(3):
            for there in range(2):
                summed = None
                for xk in range(4):
                    i = xk * 8 + slot * 2 + there
                    term = parts_ref[i, 0:64, :].astype(F32) * share[0:64, i : i + 1]
                    summed = term if summed is None else summed + term
                att_ref[there, :, slot * 128 : slot * 128 + 128] = summed.astype(BF)

    for d, y_ref in enumerate((y0, y1, y2, y3)):
        rows = pl.ds(pl.multiple_of(((z_hi + d) % 4) * 16, 16), 16)
        y_ref[...] = (
            jnp.dot(att_ref[core, rows, :], own_ref[...], preferred_element_type=F32)
            + jnp.dot(att_ref[1 - core, rows, :], other_ref[...], preferred_element_type=F32)
        ).astype(BF)


def project(at, parts, own, other):
    width = 768
    return pl.pallas_call(
        project_kernel,
        grid=(3072 // width,),
        out_shape=[jax.ShapeDtypeStruct((16, 3072), BF)] * 4,
        in_specs=[
            pl.BlockSpec(memory_space=pltpu.SMEM),
            pl.BlockSpec((32, 80, 128), lambda n: (0, 0, 0)),
            pl.BlockSpec((384, width), lambda n: (0, n)),
            pl.BlockSpec((384, width), lambda n: (0, n)),
        ],
        out_specs=[pl.BlockSpec((16, width), lambda n: (0, n))] * 4,
        scratch_shapes=[pltpu.VMEM((2, 64, 384), BF)],
        compiler_params=pltpu.CompilerParams(vmem_limit_bytes=32 * 1024 * 1024),
        name="project",
    )(at, parts, own, other)


def turn(array, axis, step):
    return lax.ppermute(array, axis, [(i, (i + step) % 4) for i in range(4)])


def local(queries, keys_in, values, block_mask, w_out):
    x, y, z = lax.axis_index("x"), lax.axis_index("y"), lax.axis_index("z_lo")
    z_hi, core = lax.axis_index("z_hi"), lax.axis_index("core")
    at = jnp.stack([x, y, jnp.minimum(z, 2), z_hi, core]).astype(jnp.int32)
    w_other = lax.ppermute(w_out, "core", [(0, 1), (1, 0)])
    packed = pack(queries, keys_in, values, block_mask.reshape(3, 64))
    mine = lax.all_to_all(packed, ("z_lo", "core", "z_hi"), split_axis=0, concat_axis=0, tiled=True)
    q, kv = spread(at, mine)
    qs = [q] + [turn(q, "x", d) for d in (1, 2, 3)]
    kv = lax.all_to_all(kv, "y", split_axis=0, concat_axis=0, tiled=True).reshape(16, 128, 256)
    parts = attend(at, qs, kv)
    parts = lax.all_to_all(parts, ("x", "z_lo", "core"), split_axis=0, concat_axis=0, tiled=True)
    ys = project(at, parts, w_out, w_other)
    summed = ys[0].astype(F32)
    for d in (1, 2, 3):
        summed = summed + turn(ys[d], "z_hi", d).astype(F32)
    return summed.astype(BF)


def solution(mesh):
    fine = Mesh(mesh.devices.reshape(4, 2, 4, 4, 4), AXES)
    tokens = P(("z_lo", "x", "y", "z_hi", "core"), None)
    placed = (
        tokens,
        tokens,
        tokens,
        P(("z_hi", "core"), ("z_lo", "x", "y"), None),
        P(("z_hi", "core"), None),
    )
    return jax.shard_map(local, mesh=fine, in_specs=placed, out_specs=tokens, check_vma=False)
```

```python
import jax
import jax.numpy as jnp
from jax import lax
from jax.experimental import pallas as pl
from jax.experimental.pallas import tpu as pltpu
from jax.sharding import Mesh, PartitionSpec as P

BF = jnp.bfloat16
F32 = jnp.float32
AXES = ("z_hi", "core", "z_lo", "x", "y")
LOW = -1e30
LOG2E = 1.4426950408889634
ROWS = 72


def pack_kernel(q_ref, k_ref, v_ref, out_ref):
    for slot in range(4):
        for core in range(2):
            for z_hi in range(4):
                head = 3 * (2 * z_hi + core) + slot
                place = slot * 8 + core * 4 + z_hi
                for part, ref in enumerate((q_ref, k_ref, v_ref)):
                    rows = slice(part * 16, part * 16 + 16)
                    if slot < 3:
                        out_ref[place, rows, :] = ref[:, head * 128 : head * 128 + 128]
                    else:
                        out_ref[place, rows, :] = jnp.zeros((16, 128), BF)


def pack(queries, keys, values):
    return pl.pallas_call(
        pack_kernel,
        out_shape=jax.ShapeDtypeStruct((32, 48, 128), BF),
        name="pack",
    )(queries, keys, values)


def spread_kernel(at_ref, m0, m1, m2, m3, in_ref, q_ref, kv_ref, held, tail, sems):
    into = pltpu.make_async_copy(in_ref, held, sems.at[0])
    into.start()
    slot, z = at_ref[2], at_ref[5]
    row = lax.broadcasted_iota(jnp.int32, (16, 64), 0)
    total = jnp.zeros((16, 64), F32)
    for d, ref in enumerate((m0, m1, m2, m3)):
        seen = ref[slot].astype(F32)
        total = total + jnp.where(row == (z + 4 - d) % 4, seen, 0.0)
    tail[...] = jnp.concatenate([total, jnp.zeros((16, 64), F32)], axis=1).astype(BF)
    into.wait()
    copies = [
        pltpu.make_async_copy(held.at[:, 16:48], kv_ref.at[there], sems.at[there])
        for there in range(4)
    ]
    copies.append(pltpu.make_async_copy(held.at[:, 0:16], q_ref.at[0:32], sems.at[4]))
    copies.append(pltpu.make_async_copy(tail, q_ref.at[32], sems.at[5]))
    for copy in copies:
        copy.start()
    for copy in copies:
        copy.wait()


def spread(at, masks, mine):
    smem = pl.BlockSpec(memory_space=pltpu.SMEM)
    vmem = pl.BlockSpec(memory_space=pltpu.VMEM)
    anywhere = pl.BlockSpec(memory_space=pl.ANY)
    return pl.pallas_call(
        spread_kernel,
        out_shape=[
            jax.ShapeDtypeStruct((33, 16, 128), BF),
            jax.ShapeDtypeStruct((4, 32, 32, 128), BF),
        ],
        in_specs=[smem, vmem, vmem, vmem, vmem, anywhere],
        out_specs=[anywhere, anywhere],
        scratch_shapes=[
            pltpu.VMEM((32, 48, 128), BF),
            pltpu.VMEM((16, 128), BF),
            pltpu.SemaphoreType.DMA((6,)),
        ],
        compiler_params=pltpu.CompilerParams(vmem_limit_bytes=56 * 1024 * 1024),
        name="spread",
    )(at, *masks, mine)


def attend_kernel(
    at_ref, q0, q1, q2, q3, kv_in, out_ref,
    q_ref, kv_ref, vt_ref, rows_ref, held, list_ref, mask_ref, sems,
):
    x = at_ref[0]
    scale = LOG2E / 128**0.5
    to_q = [pltpu.make_async_copy(q, q_ref.at[d], sems.at[d]) for d, q in enumerate((q0, q1, q2, q3))]
    to_kv = [pltpu.make_async_copy(kv_in.at[d], kv_ref.at[d], sems.at[4 + d]) for d in range(4)]
    for copy in to_q + to_kv:
        copy.start()
    for dq in range(4):
        to_q[dq].wait()
        rows_ref[dq * 8 : dq * 8 + 8, :] = q_ref[dq, 32].astype(F32)[0:8].astype(jnp.int32)
    to_scalars = pltpu.make_async_copy(rows_ref, mask_ref, sems.at[8])
    to_scalars.start()
    for yk in range(4):
        to_kv[yk].wait()
        for zk in range(4):
            value = kv_ref[yk, zk * 8 : zk * 8 + 8, 16:32, :].reshape(128, 128)
            vt_ref[yk * 4 + zk] = value.T
    to_scalars.wait()

    outs = []
    for dq in range(4):
        xq = (x + 4 - dq) % 4
        counts = []
        for zq in range(4):
            count = jnp.int32(0)
            for block in range(16):
                list_ref[zq, count] = block
                seen = mask_ref[dq * 8 + zq, (block % 4) * 16 + 4 * x + block // 4]
                count = count + jnp.where(seen > 0, 1, 0)
            counts.append(count)
        most = jnp.maximum(jnp.maximum(counts[0], counts[1]), jnp.maximum(counts[2], counts[3]))
        queries = [
            q_ref[dq, zq * 8 : zq * 8 + 8].reshape(128, 128).T for zq in range(4)
        ]

        def fold(step, states, queries=queries, counts=counts):
            after = []
            for zq in range(4):
                largest, total, acc = states[zq]
                keys, turned, biases = [], [], []
                for part in range(4):
                    place = step * 4 + part
                    here = place < counts[zq]
                    block = jnp.where(here, list_ref[zq, jnp.where(here, place, 0)], 0)
                    cut = pl.ds(pl.multiple_of((block % 4) * 8, 8), 8)
                    keys.append(kv_ref[block // 4, cut, 0:16, :].reshape(128, 128))
                    turned.append(vt_ref[block])
                    biases.append(jnp.where(here, 0.0, LOW))
                raw = jnp.dot(
                    jnp.concatenate(keys, axis=0), queries[zq], preferred_element_type=F32
                )
                scores = jnp.concatenate(
                    [raw[i * 128 : i * 128 + 128] * scale + biases[i] for i in range(4)], axis=0
                )
                new = jnp.maximum(largest, jnp.max(scores, axis=0, keepdims=True))
                weights = jnp.exp2(scores - new)
                again = jnp.exp2(largest - new)
                total = total * again + jnp.sum(weights, axis=0, keepdims=True)
                product = jnp.dot(
                    jnp.concatenate(turned, axis=1),
                    weights.astype(BF),
                    preferred_element_type=F32,
                )
                after.append((new, total, acc * again + product))
            return tuple(after)

        start = (
            jnp.full((1, 128), LOW, F32),
            jnp.zeros((1, 128), F32),
            jnp.zeros((128, 128), F32),
        )
        states = lax.fori_loop(0, (most + 3) // 4, fold, (start,) * 4)
        for zq in range(4):
            largest, total, acc = states[zq]
            empty = total == 0.0
            inverse = jnp.where(empty, 0.0, 1.0 / jnp.where(empty, 1.0, total))
            o = (acc * inverse).T.astype(BF)
            lse = largest + jnp.log2(jnp.where(empty, 1.0, total))
            hi = lse.astype(BF)
            rest = lse - hi.astype(F32)
            mid = rest.astype(BF)
            lo = (rest - mid.astype(F32)).astype(BF)
            coded = jnp.concatenate(
                [hi.astype(F32), mid.astype(F32), lo.astype(F32), jnp.zeros((5, 128), F32)], axis=0
            )
            other = jnp.concatenate([coded[:, 64:], coded[:, :64]], axis=1)
            held[dq, zq * 2, 0:64, :] = o[0:64]
            held[dq, zq * 2, 64:72, :] = coded.astype(BF)
            held[dq, zq * 2 + 1, 0:64, :] = o[64:128]
            held[dq, zq * 2 + 1, 64:72, :] = other.astype(BF)
        out = pltpu.make_async_copy(held.at[dq], out_ref.at[xq], sems.at[9 + dq])
        out.start()
        outs.append(out)
    for out in outs:
        out.wait()


def attend(at, qs, kv):
    smem = pl.BlockSpec(memory_space=pltpu.SMEM)
    anywhere = pl.BlockSpec(memory_space=pl.ANY)
    return pl.pallas_call(
        attend_kernel,
        out_shape=jax.ShapeDtypeStruct((4, 8, ROWS, 128), BF),
        in_specs=[smem] + [anywhere] * 5,
        out_specs=anywhere,
        scratch_shapes=[
            pltpu.VMEM((4, 33, 16, 128), BF),
            pltpu.VMEM((4, 32, 32, 128), BF),
            pltpu.VMEM((16, 128, 128), BF),
            pltpu.VMEM((32, 128), jnp.int32),
            pltpu.VMEM((4, 8, ROWS, 128), BF),
            pltpu.SMEM((4, 17), jnp.int32),
            pltpu.SMEM((32, 128), jnp.int32),
            pltpu.SemaphoreType.DMA((13,)),
        ],
        compiler_params=pltpu.CompilerParams(vmem_limit_bytes=56 * 1024 * 1024),
        cost_estimate=pl.CostEstimate(flops=1 << 30, bytes_accessed=2 << 20, transcendentals=1 << 21),
        name="attend",
    )(at, *qs, kv)


def project_kernel(at_ref, parts_in, own_ref, other_ref, y0, y1, y2, y3, parts_ref, att_ref, sem):
    into = pltpu.make_async_copy(parts_in, parts_ref, sem)
    into.start()
    z_hi, core = at_ref[3], at_ref[4]
    into.wait()
    coded = [parts_ref[i // 8, i % 8, 64:72, :].astype(F32) for i in range(32)]
    lse = jnp.concatenate([c[0:1] + c[1:2] + c[2:3] for c in coded], axis=0)
    groups = [lse[8 * i : 8 * i + 8] for i in range(4)]
    top = jnp.maximum(jnp.maximum(groups[0], groups[1]), jnp.maximum(groups[2], groups[3]))
    shares = [jnp.exp2(g - top) for g in groups]
    inverse = 1.0 / (shares[0] + shares[1] + shares[2] + shares[3])
    share = jnp.concatenate([s * inverse for s in shares], axis=0)
    share = jnp.concatenate([share, jnp.zeros((96, 128), F32)], axis=0).T
    for slot in range(3):
        for there in range(2):
            summed = None
            for xk in range(4):
                i = slot * 2 + there
                term = parts_ref[xk, i, 0:64, :].astype(F32) * share[0:64, xk * 8 + i : xk * 8 + i + 1]
                summed = term if summed is None else summed + term
            att_ref[there, :, slot * 128 : slot * 128 + 128] = summed.astype(BF)

    rows = [pl.ds(pl.multiple_of(((z_hi + d) % 4) * 16, 16), 16) for d in range(4)]
    own = jnp.concatenate([att_ref[core, r, :] for r in rows], axis=0)
    other = jnp.concatenate([att_ref[1 - core, r, :] for r in rows], axis=0)
    for cut in range(0, 3072, 512):
        columns = slice(cut, cut + 512)
        y = jnp.dot(own, own_ref[:, columns], preferred_element_type=F32)
        y = (y + jnp.dot(other, other_ref[:, columns], preferred_element_type=F32)).astype(BF)
        for d, y_ref in enumerate((y0, y1, y2, y3)):
            y_ref[:, columns] = y[d * 16 : d * 16 + 16]


def project(at, parts, own, other):
    vmem = pl.BlockSpec(memory_space=pltpu.VMEM)
    return pl.pallas_call(
        project_kernel,
        out_shape=[jax.ShapeDtypeStruct((16, 3072), BF)] * 4,
        in_specs=[
            pl.BlockSpec(memory_space=pltpu.SMEM),
            pl.BlockSpec(memory_space=pl.ANY),
            vmem,
            vmem,
        ],
        scratch_shapes=[
            pltpu.VMEM((4, 8, ROWS, 128), BF),
            pltpu.VMEM((2, 64, 384), BF),
            pltpu.SemaphoreType.DMA,
        ],
        compiler_params=pltpu.CompilerParams(vmem_limit_bytes=32 * 1024 * 1024),
        name="project",
    )(at, parts, own, other)


def turn(array, axis, step):
    return lax.ppermute(array, axis, [(i, (i + step) % 4) for i in range(4)])


def local(queries, keys_in, values, block_mask, w_out):
    x, y, z = lax.axis_index("x"), lax.axis_index("y"), lax.axis_index("z_lo")
    z_hi, core = lax.axis_index("z_hi"), lax.axis_index("core")
    at = jnp.stack([x, y, jnp.minimum(z, 2), z_hi, core, z]).astype(jnp.int32)
    w_other = lax.ppermute(w_out, "core", [(0, 1), (1, 0)])
    masks = [block_mask] + [turn(block_mask, "z_lo", d) for d in (1, 2, 3)]
    packed = pack(queries, keys_in, values)
    mine = lax.all_to_all(packed, ("z_lo", "core", "z_hi"), split_axis=0, concat_axis=0, tiled=True)
    q, kv = spread(at, masks, mine)
    qs = [q] + [turn(q, "x", d) for d in (1, 2, 3)]
    kv = lax.all_to_all(kv, "y", split_axis=0, concat_axis=0, tiled=True)
    parts = attend(at, qs, kv).reshape(32, ROWS, 128)
    parts = lax.all_to_all(parts, ("x", "z_lo", "core"), split_axis=0, concat_axis=0, tiled=True)
    ys = project(at, parts.reshape(4, 8, ROWS, 128), w_out, w_other)
    summed = ys[0].astype(F32)
    for d in (1, 2, 3):
        summed = summed + turn(ys[d], "z_hi", d).astype(F32)
    return summed.astype(BF)


def solution(mesh):
    fine = Mesh(mesh.devices.reshape(4, 2, 4, 4, 4), AXES)
    tokens = P(("z_lo", "x", "y", "z_hi", "core"), None)
    placed = (
        tokens,
        tokens,
        tokens,
        P(("z_hi", "core"), ("z_lo", "x", "y"), None),
        P(("z_hi", "core"), None),
    )
    return jax.shard_map(local, mesh=fine, in_specs=placed, out_specs=tokens, check_vma=False)
```

```python
import jax
import jax.numpy as jnp
from jax import lax
from jax.experimental import pallas as pl
from jax.experimental.pallas import tpu as pltpu
from jax.sharding import Mesh, PartitionSpec as P

BF = jnp.bfloat16
F32 = jnp.float32
AXES = ("z_hi", "core", "z_lo", "x", "y")
LOW = -1e30
small = pltpu.CompilerParams(vmem_limit_bytes=16 * 1024 * 1024)
LOG2E = 1.4426950408889634
ROWS = 72


def pack_kernel(q_ref, k_ref, v_ref, out_ref):
    for slot in range(4):
        for core in range(2):
            for z_hi in range(4):
                head = 3 * (2 * z_hi + core) + slot
                place = slot * 8 + core * 4 + z_hi
                for part, ref in enumerate((q_ref, k_ref, v_ref)):
                    rows = slice(part * 16, part * 16 + 16)
                    if slot < 3:
                        out_ref[place, rows, :] = ref[:, head * 128 : head * 128 + 128]
                    else:
                        out_ref[place, rows, :] = jnp.zeros((16, 128), BF)


def pack(queries, keys, values):
    return pl.pallas_call(
        pack_kernel,
        out_shape=jax.ShapeDtypeStruct((32, 48, 128), BF),
        name="pack",
    )(queries, keys, values)


def choose_kernel(at_ref, m0, m1, m2, m3, out_ref):
    slot, z = at_ref[2], at_ref[5]
    for d, ref in enumerate((m0, m1, m2, m3)):
        zq = (z + 4 - d) % 4
        for x in range(4):
            row = x * 4 + zq
            count = jnp.int32(0)
            for block in range(16):
                out_ref[row, count] = block
                seen = ref[slot, 0, (block % 4) * 16 + 4 * x + block // 4]
                count = count + jnp.where(seen > 0, 1, 0)
            out_ref[row, 16] = count


def choose(at, masks):
    smem = pl.BlockSpec(memory_space=pltpu.SMEM)
    return pl.pallas_call(
        choose_kernel,
        out_shape=jax.ShapeDtypeStruct((16, 128), jnp.int32),
        in_specs=[smem] * 5,
        out_specs=smem,
        compiler_params=small,
        name="choose",
    )(at, *masks)


def spread_kernel(lists_ref, in_ref, q_ref, kv_ref):
    lane = lax.broadcasted_iota(jnp.int32, (16, 128), 1)
    q_ref[32] = jnp.where(lane < 17, lists_ref[...], 0).astype(F32).astype(BF)
    for place in range(32):
        q_ref[place] = in_ref[place, 0:16, :]
        for there in range(4):
            kv_ref[there, place] = in_ref[place, 16:48, :]


def spread(lists, mine):
    vmem = pl.BlockSpec(memory_space=pltpu.VMEM)
    return pl.pallas_call(
        spread_kernel,
        out_shape=[
            jax.ShapeDtypeStruct((33, 16, 128), BF),
            jax.ShapeDtypeStruct((4, 32, 32, 128), BF),
        ],
        in_specs=[vmem, vmem],
        out_specs=[vmem, vmem],
        compiler_params=small,
        name="spread",
    )(lists, mine)


def attend_kernel(
    at_ref, q0, q1, q2, q3, kv_in, out_ref,
    q_ref, kv_ref, vt_ref, qt_ref, rows_ref, list_ref, sems,

):
    x = at_ref[0]
    to_q = [pltpu.make_async_copy(q, q_ref.at[d], sems.at[d]) for d, q in enumerate((q0, q1, q2, q3))]
    to_kv = [pltpu.make_async_copy(kv_in.at[d], kv_ref.at[d], sems.at[4 + d]) for d in range(4)]
    for copy in to_q + to_kv:
        copy.start()
    scale = LOG2E / 128**0.5
    for dq in range(4):
        to_q[dq].wait()
        rows_ref[dq] = q_ref[dq, 32].astype(F32).astype(jnp.int32)
    to_scalars = pltpu.make_async_copy(rows_ref, list_ref, sems.at[8])
    to_scalars.start()
    for dq in range(4):
        for zq in range(4):
            qt_ref[dq * 4 + zq] = q_ref[dq, zq * 8 : zq * 8 + 8].reshape(128, 128).T
    for yk in range(4):
        to_kv[yk].wait()
        for zk in range(4):
            value = kv_ref[yk, zk * 8 : zk * 8 + 8, 16:32, :].reshape(128, 128)
            vt_ref[yk * 4 + zk] = value.T
    to_scalars.wait()

    for dq in range(4):
        xq = (x + 4 - dq) % 4
        counts = [list_ref[dq, x * 4 + zq, 16] for zq in range(4)]
        most = jnp.maximum(jnp.maximum(counts[0], counts[1]), jnp.maximum(counts[2], counts[3]))

        def fold(step, states, dq=dq, counts=counts):
            after = []
            for zq in range(4):
                largest, total, acc = states[zq]
                keys, turned, biases = [], [], []
                for part in range(4):
                    place = step * 4 + part
                    here = place < counts[zq]
                    block = jnp.where(here, list_ref[dq, x * 4 + zq, jnp.where(here, place, 0)], 0)
                    cut = pl.ds(pl.multiple_of((block % 4) * 8, 8), 8)
                    keys.append(kv_ref[block // 4, cut, 0:16, :].reshape(128, 128))
                    turned.append(vt_ref[block])
                    biases.append(jnp.where(here, 0.0, LOW))
                raw = jnp.dot(
                    jnp.concatenate(keys, axis=0), qt_ref[dq * 4 + zq], preferred_element_type=F32
                )
                scores = jnp.concatenate(
                    [raw[i * 128 : i * 128 + 128] * scale + biases[i] for i in range(4)], axis=0
                )
                new = jnp.maximum(largest, jnp.max(scores, axis=0, keepdims=True))
                weights = jnp.exp2(scores - new)
                again = jnp.exp2(largest - new)
                total = total * again + jnp.sum(weights, axis=0, keepdims=True)
                product = jnp.dot(
                    jnp.concatenate(turned, axis=1),
                    weights.astype(BF),
                    preferred_element_type=F32,
                )
                after.append((new, total, acc * again + product))
            return tuple(after)

        start = (
            jnp.full((1, 128), LOW, F32),
            jnp.zeros((1, 128), F32),
            jnp.zeros((128, 128), F32),
        )
        states = lax.fori_loop(0, (most + 3) // 4, fold, (start,) * 4)
        for zq in range(4):
            largest, total, acc = states[zq]
            empty = total == 0.0
            inverse = jnp.where(empty, 0.0, 1.0 / jnp.where(empty, 1.0, total))
            o = (acc * inverse).T.astype(BF)
            lse = largest + jnp.log2(jnp.where(empty, 1.0, total))
            hi = lse.astype(BF)
            rest = lse - hi.astype(F32)
            mid = rest.astype(BF)
            lo = (rest - mid.astype(F32)).astype(BF)
            coded = jnp.concatenate(
                [hi.astype(F32), mid.astype(F32), lo.astype(F32), jnp.zeros((5, 128), F32)], axis=0
            )
            other = jnp.concatenate([coded[:, 64:], coded[:, :64]], axis=1)
            out_ref[xq, zq * 2, 0:64, :] = o[0:64]
            out_ref[xq, zq * 2, 64:72, :] = coded.astype(BF)
            out_ref[xq, zq * 2 + 1, 0:64, :] = o[64:128]
            out_ref[xq, zq * 2 + 1, 64:72, :] = other.astype(BF)


def attend(at, qs, kv):
    smem = pl.BlockSpec(memory_space=pltpu.SMEM)
    vmem = pl.BlockSpec(memory_space=pltpu.VMEM)
    return pl.pallas_call(
        attend_kernel,
        out_shape=jax.ShapeDtypeStruct((4, 8, ROWS, 128), BF),
        in_specs=[smem] + [pl.BlockSpec(memory_space=pl.ANY)] * 5,
        out_specs=vmem,
        scratch_shapes=[
            pltpu.VMEM((4, 33, 16, 128), BF),
            pltpu.VMEM((4, 32, 32, 128), BF),
            pltpu.VMEM((16, 128, 128), BF),
            pltpu.VMEM((16, 128, 128), BF),
            pltpu.VMEM((4, 16, 128), jnp.int32),
            pltpu.SMEM((4, 16, 128), jnp.int32),
            pltpu.SemaphoreType.DMA((9,)),
        ],
        compiler_params=small,
        cost_estimate=pl.CostEstimate(flops=1 << 30, bytes_accessed=2 << 20, transcendentals=1 << 21),
        name="attend",
    )(at, *qs, kv)


def project_kernel(at_ref, parts_ref, own_ref, other_ref, y0, y1, y2, y3, att_ref):
    z_hi, core = at_ref[3], at_ref[4]
    coded = [parts_ref[i // 8, i % 8, 64:72, :].astype(F32) for i in range(32)]
    lse = jnp.concatenate([c[0:1] + c[1:2] + c[2:3] for c in coded], axis=0)
    groups = [lse[8 * i : 8 * i + 8] for i in range(4)]
    top = jnp.maximum(jnp.maximum(groups[0], groups[1]), jnp.maximum(groups[2], groups[3]))
    shares = [jnp.exp2(g - top) for g in groups]
    inverse = 1.0 / (shares[0] + shares[1] + shares[2] + shares[3])
    share = jnp.concatenate([s * inverse for s in shares], axis=0)
    share = jnp.concatenate([share, jnp.zeros((96, 128), F32)], axis=0).T
    for slot in range(3):
        for there in range(2):
            summed = None
            for xk in range(4):
                i = slot * 2 + there
                term = parts_ref[xk, i, 0:64, :].astype(F32) * share[0:64, xk * 8 + i : xk * 8 + i + 1]
                summed = term if summed is None else summed + term
            att_ref[there, :, slot * 128 : slot * 128 + 128] = summed.astype(BF)

    rows = [pl.ds(pl.multiple_of(((z_hi + d) % 4) * 16, 16), 16) for d in range(4)]
    own = jnp.concatenate([att_ref[core, r, :] for r in rows], axis=0)
    other = jnp.concatenate([att_ref[1 - core, r, :] for r in rows], axis=0)
    for cut in range(0, 3072, 512):
        columns = slice(cut, cut + 512)
        y = jnp.dot(own, own_ref[:, columns], preferred_element_type=F32)
        y = (y + jnp.dot(other, other_ref[:, columns], preferred_element_type=F32)).astype(BF)
        for d, y_ref in enumerate((y0, y1, y2, y3)):
            y_ref[:, columns] = y[d * 16 : d * 16 + 16]


def project(at, parts, own, other):
    vmem = pl.BlockSpec(memory_space=pltpu.VMEM)
    return pl.pallas_call(
        project_kernel,
        out_shape=[jax.ShapeDtypeStruct((16, 3072), BF)] * 4,
        in_specs=[pl.BlockSpec(memory_space=pltpu.SMEM), vmem, vmem, vmem],
        out_specs=[vmem] * 4,
        scratch_shapes=[pltpu.VMEM((2, 64, 384), BF)],
        compiler_params=small,
        name="project",
    )(at, parts, own, other)


def turn(array, axis, step):
    return lax.ppermute(array, axis, [(i, (i + step) % 4) for i in range(4)])


def local(queries, keys_in, values, block_mask, w_out):
    x, y, z = lax.axis_index("x"), lax.axis_index("y"), lax.axis_index("z_lo")
    z_hi, core = lax.axis_index("z_hi"), lax.axis_index("core")
    at = jnp.stack([x, y, jnp.minimum(z, 2), z_hi, core, z]).astype(jnp.int32)
    masks = [block_mask] + [turn(block_mask, "z_lo", d) for d in (1, 2, 3)]
    lists = choose(at, masks)
    packed = pack(queries, keys_in, values)
    mine = lax.all_to_all(packed, ("z_lo", "core", "z_hi"), split_axis=0, concat_axis=0, tiled=True)
    q, kv = spread(lists, mine)
    q, w_here = lax.optimization_barrier((q, w_out))
    w_other = lax.ppermute(w_here, "core", [(0, 1), (1, 0)])
    qs = [q] + [turn(q, "x", d) for d in (1, 2, 3)]
    kv = lax.all_to_all(kv, "y", split_axis=0, concat_axis=0, tiled=True)
    parts = attend(at, qs, kv)
    parts = lax.all_to_all(
        parts.reshape(32, ROWS, 128), ("x", "z_lo", "core"), split_axis=0, concat_axis=0, tiled=True
    )
    ys = project(at, parts.reshape(4, 8, ROWS, 128), w_out, w_other)
    far, right, left = [turn(ys[d], "z_hi", d).astype(F32) for d in (2, 1, 3)]
    return (((ys[0].astype(F32) + far) + right) + left).astype(BF)


def solution(mesh):
    fine = Mesh(mesh.devices.reshape(4, 2, 4, 4, 4), AXES)
    tokens = P(("z_lo", "x", "y", "z_hi", "core"), None)
    placed = (
        tokens,
        tokens,
        tokens,
        P(("z_hi", "core"), ("z_lo", "x", "y"), None),
        P(("z_hi", "core"), None),
    )
    return jax.shard_map(local, mesh=fine, in_specs=placed, out_specs=tokens, check_vma=False)
```

```python
import jax
import jax.numpy as jnp
from jax import lax
from jax.experimental import pallas as pl
from jax.experimental.pallas import tpu as pltpu
from jax.sharding import Mesh, PartitionSpec as P

BF = jnp.bfloat16
F32 = jnp.float32
AXES = ("z_hi", "core", "z_lo", "x", "y")
LOW = -1e30
small = pltpu.CompilerParams(vmem_limit_bytes=16 * 1024 * 1024)
LOG2E = 1.4426950408889634
ROWS = 72


def pack_kernel(q_in, k_in, v_in, out_ref, q_ref, k_ref, v_ref, held, sems):
    parts = ((q_in, q_ref), (k_in, k_ref), (v_in, v_ref))
    into = [pltpu.make_async_copy(a, b, sems.at[i]) for i, (a, b) in enumerate(parts)]
    for copy in into:
        copy.start()
    held[24:32] = jnp.zeros((8, 48, 128), BF)
    outs = [pltpu.make_async_copy(held.at[24:32], out_ref.at[24:32], sems.at[3])]
    outs[0].start()
    for part, (_, ref) in enumerate(parts):
        rows = slice(part * 16, part * 16 + 16)
        into[part].wait()
        for slot in range(3):
            for core in range(2):
                for z_hi in range(4):
                    head = 3 * (2 * z_hi + core) + slot
                    held[slot * 8 + core * 4 + z_hi, rows, :] = ref[:, head * 128 : head * 128 + 128]
        outs.append(
            pltpu.make_async_copy(held.at[0:24, rows], out_ref.at[0:24, rows], sems.at[4 + part])
        )
        outs[-1].start()
    for copy in outs:
        copy.wait()


def pack(queries, keys, values):
    anywhere = pl.BlockSpec(memory_space=pl.ANY)
    return pl.pallas_call(
        pack_kernel,
        out_shape=jax.ShapeDtypeStruct((32, 48, 128), BF),
        in_specs=[anywhere] * 3,
        out_specs=anywhere,
        scratch_shapes=[pltpu.VMEM((16, 3072), BF)] * 3
        + [pltpu.VMEM((32, 48, 128), BF), pltpu.SemaphoreType.DMA((7,))],
        compiler_params=pltpu.CompilerParams(vmem_limit_bytes=56 * 1024 * 1024),
        name="pack",
    )(queries, keys, values)


def choose_kernel(mask_ref, out_ref):
    for slot in range(3):
        for x in range(4):
            count = jnp.int32(0)
            for block in range(16):
                out_ref[slot, x, count] = block
                seen = mask_ref[slot, 0, (block % 4) * 16 + 4 * x + block // 4]
                count = count + jnp.where(seen > 0, 1, 0)
            out_ref[slot, x, 16] = count


def choose(mask):
    smem = pl.BlockSpec(memory_space=pltpu.SMEM)
    return pl.pallas_call(
        choose_kernel,
        out_shape=jax.ShapeDtypeStruct((3, 8, 128), jnp.int32),
        in_specs=[smem],
        out_specs=smem,
        compiler_params=small,
        name="choose",
    )(mask)


def spread_kernel(at_ref, l0, l1, l2, l3, in_ref, q_ref, kv_ref, tail):
    slot, z = at_ref[2], at_ref[5]
    used = lax.broadcasted_iota(jnp.int32, (8, 128), 0) < 4
    used = used & (lax.broadcasted_iota(jnp.int32, (8, 128), 1) < 17)
    for d, ref in enumerate((l0, l1, l2, l3)):
        tail[(z + 4 - d) % 4] = jnp.where(used, ref[slot], 0).astype(F32)
    q_ref[32:34] = tail[...].reshape(2, 16, 128).astype(BF)
    for place in range(32):
        q_ref[place] = in_ref[place, 0:16, :]
        for there in range(4):
            kv_ref[there, place] = in_ref[place, 16:48, :]


def spread(at, lists, mine):
    vmem = pl.BlockSpec(memory_space=pltpu.VMEM)
    return pl.pallas_call(
        spread_kernel,
        out_shape=[
            jax.ShapeDtypeStruct((34, 16, 128), BF),
            jax.ShapeDtypeStruct((4, 32, 32, 128), BF),
        ],
        in_specs=[pl.BlockSpec(memory_space=pltpu.SMEM)] + [vmem] * 5,
        out_specs=[vmem, vmem],
        scratch_shapes=[pltpu.VMEM((4, 8, 128), F32)],
        compiler_params=small,
        name="spread",
    )(at, *lists, mine)


def attend_kernel(
    at_ref, q0, q1, q2, q3, kv_in, out_ref,
    q_ref, kv_ref, vt_ref, qt_ref, sums_ref, acc_ref, rows_ref, list_ref, sems,

):
    x = at_ref[0]
    to_q = [pltpu.make_async_copy(q, q_ref.at[d], sems.at[d]) for d, q in enumerate((q0, q1, q2, q3))]
    to_kv = [pltpu.make_async_copy(kv_in.at[d], kv_ref.at[d], sems.at[4 + d]) for d in range(4)]
    for copy in to_q + to_kv:
        copy.start()
    scale = LOG2E / 128**0.5
    for dq in range(4):
        to_q[dq].wait()
        rows_ref[dq] = q_ref[dq, 32:34].reshape(32, 128).astype(F32).astype(jnp.int32)
    to_scalars = pltpu.make_async_copy(rows_ref, list_ref, sems.at[8])
    to_scalars.start()
    for dq in range(4):
        for zq in range(4):
            qt_ref[dq * 4 + zq] = q_ref[dq, zq * 8 : zq * 8 + 8].reshape(128, 128).T
    for yk in range(4):
        to_kv[yk].wait()
        for zk in range(4):
            value = kv_ref[yk, zk * 8 : zk * 8 + 8, 16:32, :].reshape(128, 128)
            vt_ref[yk * 4 + zk] = value.T
    to_scalars.wait()

    counts = [list_ref[at // 4, at % 4 * 8 + x, 16] for at in range(16)]

    def look(at, step, state):
        keys, turned, biases = [], [], []
        for part in range(4):
            place = step * 4 + part
            here = place < counts[at]
            block = jnp.where(here, list_ref[at // 4, at % 4 * 8 + x, jnp.where(here, place, 0)], 0)
            cut = pl.ds(pl.multiple_of((block % 4) * 8, 8), 8)
            keys.append(kv_ref[block // 4, cut, 0:16, :].reshape(128, 128))
            turned.append(vt_ref[block])
            biases.append(jnp.where(here, 0.0, LOW))
        raw = jnp.dot(jnp.concatenate(keys, axis=0), qt_ref[at], preferred_element_type=F32)
        scores = jnp.concatenate(
            [raw[i * 128 : i * 128 + 128] * scale + biases[i] for i in range(4)], axis=0
        )
        new = jnp.max(scores, axis=0, keepdims=True)
        if state is not None:
            new = jnp.maximum(state[0], new)
        weights = jnp.exp2(scores - new)
        total = jnp.sum(weights, axis=0, keepdims=True)
        acc = jnp.dot(
            jnp.concatenate(turned, axis=1), weights.astype(BF), preferred_element_type=F32
        )
        if state is not None:
            again = jnp.exp2(state[0] - new)
            total = state[1] * again + total
            acc = state[2] * again + acc
        return new, total, acc

    def keep(at, state):
        sums_ref[at, 0:1, :] = state[0]
        sums_ref[at, 1:2, :] = state[1]
        acc_ref[at] = state[2]

    def kept(at):
        return sums_ref[at, 0:1, :], sums_ref[at, 1:2, :], acc_ref[at]

    for at in range(16):
        keep(at, look(at, 0, None))

    for group in range(4):
        ats = range(group * 4, group * 4 + 4)
        most = counts[ats[0]]
        for at in ats[1:]:
            most = jnp.maximum(most, counts[at])

        @pl.loop(1, (most + 3) // 4)
        def _(step, ats=ats):
            for at in ats:
                keep(at, look(at, step, kept(at)))

    for at in range(16):
        largest, total, acc = kept(at)
        xq, zq = (x + 4 - at // 4) % 4, at % 4
        o = (acc * (1.0 / total)).T.astype(BF)
        lse = jnp.where(counts[at] > 0, largest + jnp.log2(total), LOW)
        hi = lse.astype(BF)
        rest = lse - hi.astype(F32)
        mid = rest.astype(BF)
        lo = (rest - mid.astype(F32)).astype(BF)
        coded = jnp.concatenate(
            [hi.astype(F32), mid.astype(F32), lo.astype(F32), jnp.zeros((5, 128), F32)], axis=0
        )
        other = jnp.concatenate([coded[:, 64:], coded[:, :64]], axis=1)
        out_ref[xq, zq * 2, 0:64, :] = o[0:64]
        out_ref[xq, zq * 2, 64:72, :] = coded.astype(BF)
        out_ref[xq, zq * 2 + 1, 0:64, :] = o[64:128]
        out_ref[xq, zq * 2 + 1, 64:72, :] = other.astype(BF)


def attend(at, qs, kv):
    smem = pl.BlockSpec(memory_space=pltpu.SMEM)
    vmem = pl.BlockSpec(memory_space=pltpu.VMEM)
    return pl.pallas_call(
        attend_kernel,
        out_shape=jax.ShapeDtypeStruct((4, 8, ROWS, 128), BF),
        in_specs=[smem] + [pl.BlockSpec(memory_space=pl.ANY)] * 5,
        out_specs=vmem,
        scratch_shapes=[
            pltpu.VMEM((4, 34, 16, 128), BF),
            pltpu.VMEM((4, 32, 32, 128), BF),
            pltpu.VMEM((16, 128, 128), BF),
            pltpu.VMEM((16, 128, 128), BF),
            pltpu.VMEM((16, 8, 128), F32),
            pltpu.VMEM((16, 128, 128), F32),
            pltpu.VMEM((4, 32, 128), jnp.int32),
            pltpu.SMEM((4, 32, 128), jnp.int32),
            pltpu.SemaphoreType.DMA((9,)),
        ],
        compiler_params=pltpu.CompilerParams(vmem_limit_bytes=44 * 1024 * 1024),
        cost_estimate=pl.CostEstimate(flops=1 << 30, bytes_accessed=2 << 20, transcendentals=1 << 21),
        name="attend",
    )(at, *qs, kv)


def project_kernel(at_ref, parts_ref, own_in, other_in, y0, y1, y2, y3, att_ref, own_ref, other_ref, sems):
    arriving = []
    for cut in range(6):
        columns = slice(cut * 512, cut * 512 + 512)
        for i, (a, b) in enumerate(((own_in, own_ref), (other_in, other_ref))):
            copy = pltpu.make_async_copy(a.at[:, columns], b.at[:, columns], sems.at[i, cut])
            copy.start()
            arriving.append(copy)
    z_hi, core = at_ref[3], at_ref[4]
    coded = [parts_ref[i // 8, i % 8, 64:72, :].astype(F32) for i in range(32)]
    lse = jnp.concatenate([c[0:1] + c[1:2] + c[2:3] for c in coded], axis=0)
    groups = [lse[8 * i : 8 * i + 8] for i in range(4)]
    top = jnp.maximum(jnp.maximum(groups[0], groups[1]), jnp.maximum(groups[2], groups[3]))
    shares = [jnp.exp2(g - top) for g in groups]
    inverse = 1.0 / (shares[0] + shares[1] + shares[2] + shares[3])
    share = jnp.concatenate([s * inverse for s in shares], axis=0)
    share = jnp.concatenate([share, jnp.zeros((96, 128), F32)], axis=0).T
    for slot in range(3):
        for there in range(2):
            summed = None
            for xk in range(4):
                i = slot * 2 + there
                term = parts_ref[xk, i, 0:64, :].astype(F32) * share[0:64, xk * 8 + i : xk * 8 + i + 1]
                summed = term if summed is None else summed + term
            att_ref[there, :, slot * 128 : slot * 128 + 128] = summed.astype(BF)

    rows = [pl.ds(pl.multiple_of(((z_hi + d) % 4) * 16, 16), 16) for d in range(4)]
    own = jnp.concatenate([att_ref[core, r, :] for r in rows], axis=0)
    other = jnp.concatenate([att_ref[1 - core, r, :] for r in rows], axis=0)
    for cut in range(0, 3072, 512):
        columns = slice(cut, cut + 512)
        arriving[cut // 256].wait()
        arriving[cut // 256 + 1].wait()
        y = jnp.dot(own, own_ref[:, columns], preferred_element_type=F32)
        y = (y + jnp.dot(other, other_ref[:, columns], preferred_element_type=F32)).astype(BF)
        for d, y_ref in enumerate((y0, y1, y2, y3)):
            y_ref[:, columns] = y[d * 16 : d * 16 + 16]


def project(at, parts, own, other):
    vmem = pl.BlockSpec(memory_space=pltpu.VMEM)
    return pl.pallas_call(
        project_kernel,
        out_shape=[jax.ShapeDtypeStruct((16, 3072), BF)] * 4,
        in_specs=[
            pl.BlockSpec(memory_space=pltpu.SMEM),
            vmem,
            pl.BlockSpec(memory_space=pl.ANY),
            pl.BlockSpec(memory_space=pl.ANY),
        ],
        out_specs=[vmem] * 4,
        scratch_shapes=[
            pltpu.VMEM((2, 64, 384), BF),
            pltpu.VMEM((384, 3072), BF),
            pltpu.VMEM((384, 3072), BF),
            pltpu.SemaphoreType.DMA((2, 6)),
        ],
        compiler_params=small,
        name="project",
    )(at, parts, own, other)


def turn(array, axis, step):
    return lax.ppermute(array, axis, [(i, (i + step) % 4) for i in range(4)])


def local(queries, keys_in, values, block_mask, w_out):
    x, y, z = lax.axis_index("x"), lax.axis_index("y"), lax.axis_index("z_lo")
    z_hi, core = lax.axis_index("z_hi"), lax.axis_index("core")
    at = jnp.stack([x, y, jnp.minimum(z, 2), z_hi, core, z]).astype(jnp.int32)
    chosen = choose(block_mask)
    lists = [chosen] + [turn(chosen, "z_lo", d) for d in (1, 2, 3)]
    packed = pack(queries, keys_in, values)
    mine = lax.all_to_all(packed, ("z_lo", "core", "z_hi"), split_axis=0, concat_axis=0, tiled=True)
    q, kv = spread(at, lists, mine)
    q, w_here = lax.optimization_barrier((q, w_out))
    w_other = lax.ppermute(w_here, "core", [(0, 1), (1, 0)])
    qs = [q] + [turn(q, "x", d) for d in (1, 2, 3)]
    kv = lax.all_to_all(kv, "y", split_axis=0, concat_axis=0, tiled=True)
    parts = attend(at, qs, kv)
    parts = lax.all_to_all(
        parts.reshape(32, ROWS, 128), ("x", "z_lo", "core"), split_axis=0, concat_axis=0, tiled=True
    )
    ys = project(at, parts.reshape(4, 8, ROWS, 128), w_out, w_other)
    far, right, left = [turn(ys[d], "z_hi", d).astype(F32) for d in (2, 1, 3)]
    return (((ys[0].astype(F32) + far) + right) + left).astype(BF)


def solution(mesh):
    fine = Mesh(mesh.devices.reshape(4, 2, 4, 4, 4), AXES)
    tokens = P(("z_lo", "x", "y", "z_hi", "core"), None)
    placed = (
        tokens,
        tokens,
        tokens,
        P(("z_hi", "core"), ("z_lo", "x", "y"), None),
        P(("z_hi", "core"), None),
    )
    return jax.shard_map(local, mesh=fine, in_specs=placed, out_specs=tokens, check_vma=False)
```

```python
import jax
import jax.numpy as jnp
from jax import lax
from jax.experimental import pallas as pl
from jax.experimental.pallas import tpu as pltpu
from jax.sharding import Mesh, PartitionSpec as P

BF = jnp.bfloat16
F32 = jnp.float32
AXES = ("z_hi", "core", "z_lo", "x", "y")
LOW = -1e30
small = pltpu.CompilerParams(vmem_limit_bytes=16 * 1024 * 1024)
LOG2E = 1.4426950408889634
ROWS = 72


def pack_kernel(q_in, k_in, v_in, out_ref, q_ref, k_ref, v_ref, held, sems):
    parts = ((q_in, q_ref), (k_in, k_ref), (v_in, v_ref))
    into = [pltpu.make_async_copy(a, b, sems.at[i]) for i, (a, b) in enumerate(parts)]
    for copy in into:
        copy.start()
    held[24:32] = jnp.zeros((8, 48, 128), BF)
    outs = [pltpu.make_async_copy(held.at[24:32], out_ref.at[24:32], sems.at[3])]
    outs[0].start()
    for part, (_, ref) in enumerate(parts):
        rows = slice(part * 16, part * 16 + 16)
        into[part].wait()
        for slot in range(3):
            for core in range(2):
                for z_hi in range(4):
                    head = 3 * (2 * z_hi + core) + slot
                    held[slot * 8 + core * 4 + z_hi, rows, :] = ref[:, head * 128 : head * 128 + 128]
        outs.append(
            pltpu.make_async_copy(held.at[0:24, rows], out_ref.at[0:24, rows], sems.at[4 + part])
        )
        outs[-1].start()
    for copy in outs:
        copy.wait()


def pack(queries, keys, values):
    anywhere = pl.BlockSpec(memory_space=pl.ANY)
    return pl.pallas_call(
        pack_kernel,
        out_shape=jax.ShapeDtypeStruct((32, 48, 128), BF),
        in_specs=[anywhere] * 3,
        out_specs=anywhere,
        scratch_shapes=[pltpu.VMEM((16, 3072), BF)] * 3
        + [pltpu.VMEM((32, 48, 128), BF), pltpu.SemaphoreType.DMA((7,))],
        compiler_params=pltpu.CompilerParams(vmem_limit_bytes=56 * 1024 * 1024),
        name="pack",
    )(queries, keys, values)


def choose_kernel(mask_ref, out_ref):
    for slot in range(3):
        for x in range(4):
            count = jnp.int32(0)
            for block in range(16):
                out_ref[slot, x, count] = block
                seen = mask_ref[slot, 0, (block % 4) * 16 + 4 * x + block // 4]
                count = count + jnp.where(seen > 0, 1, 0)
            out_ref[slot, x, 16] = count


def choose(mask):
    smem = pl.BlockSpec(memory_space=pltpu.SMEM)
    return pl.pallas_call(
        choose_kernel,
        out_shape=jax.ShapeDtypeStruct((3, 8, 128), jnp.int32),
        in_specs=[smem],
        out_specs=smem,
        compiler_params=small,
        name="choose",
    )(mask)


def spread_kernel(at_ref, l0, l1, l2, l3, in_ref, q_ref, kv_ref, tail):
    slot, z = at_ref[2], at_ref[5]
    used = lax.broadcasted_iota(jnp.int32, (8, 128), 0) < 4
    used = used & (lax.broadcasted_iota(jnp.int32, (8, 128), 1) < 17)
    for d, ref in enumerate((l0, l1, l2, l3)):
        tail[(z + 4 - d) % 4] = jnp.where(used, ref[slot], 0).astype(F32)
    q_ref[32:34] = tail[...].reshape(2, 16, 128).astype(BF)
    for place in range(32):
        q_ref[place] = in_ref[place, 0:16, :]
        for there in range(4):
            kv_ref[there, place] = in_ref[place, 16:48, :]


def spread(at, lists, mine):
    vmem = pl.BlockSpec(memory_space=pltpu.VMEM)
    return pl.pallas_call(
        spread_kernel,
        out_shape=[
            jax.ShapeDtypeStruct((34, 16, 128), BF),
            jax.ShapeDtypeStruct((4, 32, 32, 128), BF),
        ],
        in_specs=[pl.BlockSpec(memory_space=pltpu.SMEM)] + [vmem] * 5,
        out_specs=[vmem, vmem],
        scratch_shapes=[pltpu.VMEM((4, 8, 128), F32)],
        compiler_params=small,
        name="spread",
    )(at, *lists, mine)


def attend_kernel(
    at_ref, q0, q1, q2, q3, kv_in, out_ref,
    q_ref, kv_ref, vt_ref, qt_ref, sums_ref, acc_ref, rows_ref, list_ref, sems,

):
    x, core = at_ref[0], at_ref[4]
    to_q = [pltpu.make_async_copy(q, q_ref.at[d], sems.at[d]) for d, q in enumerate((q0, q1, q2, q3))]
    to_kv = [pltpu.make_async_copy(kv_in.at[d], kv_ref.at[d], sems.at[4 + d]) for d in range(4)]
    for copy in to_q + to_kv:
        copy.start()
    scale = LOG2E / 128**0.5
    for dq in range(4):
        to_q[dq].wait()
        rows_ref[dq] = q_ref[dq, 32:34].reshape(32, 128).astype(F32).astype(jnp.int32)
    to_scalars = pltpu.make_async_copy(rows_ref, list_ref, sems.at[8])
    to_scalars.start()
    for dq in range(4):
        for zq in range(4):
            qt_ref[dq * 4 + zq] = q_ref[dq, zq * 8 : zq * 8 + 8].reshape(128, 128).T
    for yk in range(4):
        to_kv[yk].wait()
        for zk in range(4):
            value = kv_ref[yk, zk * 8 : zk * 8 + 8, 16:32, :].reshape(128, 128)
            vt_ref[yk * 4 + zk] = value.T
    to_scalars.wait()

    counts = [list_ref[at // 4, at % 4 * 8 + x, 16] for at in range(16)]

    def look(at, step, state):
        keys, turned, biases = [], [], []
        for part in range(4):
            place = step * 4 + part
            here = place < counts[at]
            block = jnp.where(here, list_ref[at // 4, at % 4 * 8 + x, jnp.where(here, place, 0)], 0)
            cut = pl.ds(pl.multiple_of((block % 4) * 8, 8), 8)
            keys.append(kv_ref[block // 4, cut, 0:16, :].reshape(128, 128))
            turned.append(vt_ref[block])
            biases.append(jnp.where(here, 0.0, LOW))
        raw = jnp.dot(jnp.concatenate(keys, axis=0), qt_ref[at], preferred_element_type=F32)
        scores = jnp.concatenate(
            [raw[i * 128 : i * 128 + 128] * scale + biases[i] for i in range(4)], axis=0
        )
        new = jnp.max(scores, axis=0, keepdims=True)
        if state is not None:
            new = jnp.maximum(state[0], new)
        weights = jnp.exp2(scores - new)
        total = jnp.sum(weights, axis=0, keepdims=True)
        acc = jnp.dot(
            jnp.concatenate(turned, axis=1), weights.astype(BF), preferred_element_type=F32
        )
        if state is not None:
            again = jnp.exp2(state[0] - new)
            total = state[1] * again + total
            acc = state[2] * again + acc
        return new, total, acc

    def keep(at, state):
        sums_ref[at, 0:1, :] = state[0]
        sums_ref[at, 1:2, :] = state[1]
        acc_ref[at] = state[2]

    def kept(at):
        return sums_ref[at, 0:1, :], sums_ref[at, 1:2, :], acc_ref[at]

    for at in range(16):
        keep(at, look(at, 0, None))

    for group in range(4):
        ats = range(group * 4, group * 4 + 4)
        most = counts[ats[0]]
        for at in ats[1:]:
            most = jnp.maximum(most, counts[at])

        @pl.loop(1, (most + 3) // 4)
        def _(step, ats=ats):
            for at in ats:
                keep(at, look(at, step, kept(at)))

    for at in range(16):
        largest, total, acc = kept(at)
        xq, zq = (x + jnp.where(core == 0, 4 - at // 4, at // 4)) % 4, at % 4
        o = (acc * (1.0 / total)).T.astype(BF)
        lse = jnp.where(counts[at] > 0, largest + jnp.log2(total), LOW)
        hi = lse.astype(BF)
        rest = lse - hi.astype(F32)
        mid = rest.astype(BF)
        lo = (rest - mid.astype(F32)).astype(BF)
        coded = jnp.concatenate(
            [hi.astype(F32), mid.astype(F32), lo.astype(F32), jnp.zeros((5, 128), F32)], axis=0
        )
        other = jnp.concatenate([coded[:, 64:], coded[:, :64]], axis=1)
        out_ref[xq, zq * 2, 0:64, :] = o[0:64]
        out_ref[xq, zq * 2, 64:72, :] = coded.astype(BF)
        out_ref[xq, zq * 2 + 1, 0:64, :] = o[64:128]
        out_ref[xq, zq * 2 + 1, 64:72, :] = other.astype(BF)


def attend(at, qs, kv):
    smem = pl.BlockSpec(memory_space=pltpu.SMEM)
    vmem = pl.BlockSpec(memory_space=pltpu.VMEM)
    return pl.pallas_call(
        attend_kernel,
        out_shape=jax.ShapeDtypeStruct((4, 8, ROWS, 128), BF),
        in_specs=[smem] + [pl.BlockSpec(memory_space=pl.ANY)] * 5,
        out_specs=vmem,
        scratch_shapes=[
            pltpu.VMEM((4, 34, 16, 128), BF),
            pltpu.VMEM((4, 32, 32, 128), BF),
            pltpu.VMEM((16, 128, 128), BF),
            pltpu.VMEM((16, 128, 128), BF),
            pltpu.VMEM((16, 8, 128), F32),
            pltpu.VMEM((16, 128, 128), F32),
            pltpu.VMEM((4, 32, 128), jnp.int32),
            pltpu.SMEM((4, 32, 128), jnp.int32),
            pltpu.SemaphoreType.DMA((9,)),
        ],
        compiler_params=pltpu.CompilerParams(vmem_limit_bytes=44 * 1024 * 1024),
        cost_estimate=pl.CostEstimate(flops=1 << 30, bytes_accessed=2 << 20, transcendentals=1 << 21),
        name="attend",
    )(at, *qs, kv)


def project_kernel(at_ref, parts_ref, own_in, other_in, y0, y1, y2, y3, att_ref, own_ref, other_ref, sems):
    arriving = []
    for cut in range(6):
        columns = slice(cut * 512, cut * 512 + 512)
        for i, (a, b) in enumerate(((own_in, own_ref), (other_in, other_ref))):
            copy = pltpu.make_async_copy(a.at[:, columns], b.at[:, columns], sems.at[i, cut])
            copy.start()
            arriving.append(copy)
    z_hi, core = at_ref[3], at_ref[4]
    coded = [parts_ref[i // 8, i % 8, 64:72, :].astype(F32) for i in range(32)]
    lse = jnp.concatenate([c[0:1] + c[1:2] + c[2:3] for c in coded], axis=0)
    groups = [lse[8 * i : 8 * i + 8] for i in range(4)]
    top = jnp.maximum(jnp.maximum(groups[0], groups[1]), jnp.maximum(groups[2], groups[3]))
    shares = [jnp.exp2(g - top) for g in groups]
    inverse = 1.0 / (shares[0] + shares[1] + shares[2] + shares[3])
    share = jnp.concatenate([s * inverse for s in shares], axis=0)
    share = jnp.concatenate([share, jnp.zeros((96, 128), F32)], axis=0).T
    for slot in range(3):
        for there in range(2):
            summed = None
            for xk in range(4):
                i = slot * 2 + there
                term = parts_ref[xk, i, 0:64, :].astype(F32) * share[0:64, xk * 8 + i : xk * 8 + i + 1]
                summed = term if summed is None else summed + term
            att_ref[there, :, slot * 128 : slot * 128 + 128] = summed.astype(BF)

    rows = []
    for d in range(4):
        there = (z_hi + jnp.where(core == 0, d, 4 - d)) % 4
        rows.append(pl.ds(pl.multiple_of(there * 16, 16), 16))
    own = jnp.concatenate([att_ref[core, r, :] for r in rows], axis=0)
    other = jnp.concatenate([att_ref[1 - core, r, :] for r in rows], axis=0)
    for cut in range(0, 3072, 512):
        columns = slice(cut, cut + 512)
        arriving[cut // 256].wait()
        arriving[cut // 256 + 1].wait()
        y = jnp.dot(own, own_ref[:, columns], preferred_element_type=F32)
        y = (y + jnp.dot(other, other_ref[:, columns], preferred_element_type=F32)).astype(BF)
        for d, y_ref in enumerate((y0, y1, y2, y3)):
            y_ref[:, columns] = y[d * 16 : d * 16 + 16]


def project(at, parts, own, other):
    vmem = pl.BlockSpec(memory_space=pltpu.VMEM)
    return pl.pallas_call(
        project_kernel,
        out_shape=[jax.ShapeDtypeStruct((16, 3072), BF)] * 4,
        in_specs=[
            pl.BlockSpec(memory_space=pltpu.SMEM),
            vmem,
            pl.BlockSpec(memory_space=pl.ANY),
            pl.BlockSpec(memory_space=pl.ANY),
        ],
        out_specs=[vmem] * 4,
        scratch_shapes=[
            pltpu.VMEM((2, 64, 384), BF),
            pltpu.VMEM((384, 3072), BF),
            pltpu.VMEM((384, 3072), BF),
            pltpu.SemaphoreType.DMA((2, 6)),
        ],
        compiler_params=small,
        name="project",
    )(at, parts, own, other)


def turn(array, axis, step):
    return lax.ppermute(array, axis, [(i, (i + step) % 4) for i in range(4)])


def turn_apart(array, axis, step):
    names = (axis, "core") if axis == "z_hi" else ("core", axis)
    pairs = []
    for core in range(2):
        for i in range(4):
            j = (i + (step if core == 0 else -step)) % 4
            pairs.append((2 * i + core, 2 * j + core) if axis == "z_hi" else (4 * core + i, 4 * core + j))
    return lax.ppermute(array, names, pairs)


def local(queries, keys_in, values, block_mask, w_out):
    x, y, z = lax.axis_index("x"), lax.axis_index("y"), lax.axis_index("z_lo")
    z_hi, core = lax.axis_index("z_hi"), lax.axis_index("core")
    at = jnp.stack([x, y, jnp.minimum(z, 2), z_hi, core, z]).astype(jnp.int32)
    chosen = choose(block_mask)
    lists = [chosen] + [turn(chosen, "z_lo", d) for d in (1, 2, 3)]
    packed = pack(queries, keys_in, values)
    mine = lax.all_to_all(packed, ("z_lo", "core", "z_hi"), split_axis=0, concat_axis=0, tiled=True)
    q, kv = spread(at, lists, mine)
    q, w_here = lax.optimization_barrier((q, w_out))
    w_other = lax.ppermute(w_here, "core", [(0, 1), (1, 0)])
    qs = [q] + [turn_apart(q, "x", d) for d in (1, 2, 3)]
    kv = lax.all_to_all(kv, "y", split_axis=0, concat_axis=0, tiled=True)
    parts = attend(at, qs, kv)
    parts = lax.all_to_all(
        parts.reshape(32, ROWS, 128), ("x", "z_lo", "core"), split_axis=0, concat_axis=0, tiled=True
    )
    ys = project(at, parts.reshape(4, 8, ROWS, 128), w_out, w_other)
    far, right, left = [turn_apart(ys[d], "z_hi", d).astype(F32) for d in (2, 1, 3)]
    return (((ys[0].astype(F32) + far) + right) + left).astype(BF)


def solution(mesh):
    fine = Mesh(mesh.devices.reshape(4, 2, 4, 4, 4), AXES)
    tokens = P(("z_lo", "x", "y", "z_hi", "core"), None)
    placed = (
        tokens,
        tokens,
        tokens,
        P(("z_hi", "core"), ("z_lo", "x", "y"), None),
        P(("z_hi", "core"), None),
    )
    return jax.shard_map(local, mesh=fine, in_specs=placed, out_specs=tokens, check_vma=False)
```

```python
import jax
import jax.numpy as jnp
from jax import lax
from jax.experimental import pallas as pl
from jax.experimental.pallas import tpu as pltpu
from jax.sharding import Mesh, PartitionSpec as P

BF = jnp.bfloat16
F32 = jnp.float32
AXES = ("z_hi", "core", "z_lo", "x", "y")
LOW = -1e30
small = pltpu.CompilerParams(vmem_limit_bytes=16 * 1024 * 1024)
LOG2E = 1.4426950408889634
ROWS = 72


def pack_kernel(q_in, k_in, v_in, out_ref, q_ref, k_ref, v_ref, held, sems):
    parts = ((q_in, q_ref), (k_in, k_ref), (v_in, v_ref))
    into = [pltpu.make_async_copy(a, b, sems.at[i]) for i, (a, b) in enumerate(parts)]
    for copy in into:
        copy.start()
    held[24:32] = jnp.zeros((8, 48, 128), BF)
    outs = [pltpu.make_async_copy(held.at[24:32], out_ref.at[24:32], sems.at[3])]
    outs[0].start()
    for part, (_, ref) in enumerate(parts):
        rows = slice(part * 16, part * 16 + 16)
        into[part].wait()
        for slot in range(3):
            for core in range(2):
                for z_hi in range(4):
                    head = 3 * (2 * z_hi + core) + slot
                    held[slot * 8 + core * 4 + z_hi, rows, :] = ref[:, head * 128 : head * 128 + 128]
        outs.append(
            pltpu.make_async_copy(held.at[0:24, rows], out_ref.at[0:24, rows], sems.at[4 + part])
        )
        outs[-1].start()
    for copy in outs:
        copy.wait()


def pack(queries, keys, values):
    anywhere = pl.BlockSpec(memory_space=pl.ANY)
    return pl.pallas_call(
        pack_kernel,
        out_shape=jax.ShapeDtypeStruct((32, 48, 128), BF),
        in_specs=[anywhere] * 3,
        out_specs=anywhere,
        scratch_shapes=[pltpu.VMEM((16, 3072), BF)] * 3
        + [pltpu.VMEM((32, 48, 128), BF), pltpu.SemaphoreType.DMA((7,))],
        compiler_params=pltpu.CompilerParams(vmem_limit_bytes=56 * 1024 * 1024),
        name="pack",
    )(queries, keys, values)


def choose_kernel(mask_ref, out_ref):
    for slot in range(3):
        for x in range(4):
            count = jnp.int32(0)
            for block in range(16):
                out_ref[slot, x, count] = block
                seen = mask_ref[slot, 0, (block % 4) * 16 + 4 * x + block // 4]
                count = count + jnp.where(seen > 0, 1, 0)
            out_ref[slot, x, 16] = count


def choose(mask):
    smem = pl.BlockSpec(memory_space=pltpu.SMEM)
    return pl.pallas_call(
        choose_kernel,
        out_shape=jax.ShapeDtypeStruct((3, 8, 128), jnp.int32),
        in_specs=[smem],
        out_specs=smem,
        compiler_params=small,
        name="choose",
    )(mask)


def spread_kernel(at_ref, l0, l1, l2, l3, in_ref, q_ref, kv_ref, tail):
    slot, z = at_ref[2], at_ref[5]
    used = lax.broadcasted_iota(jnp.int32, (8, 128), 0) < 4
    used = used & (lax.broadcasted_iota(jnp.int32, (8, 128), 1) < 17)
    for d, ref in enumerate((l0, l1, l2, l3)):
        tail[(z + 4 - d) % 4] = jnp.where(used, ref[slot], 0).astype(F32)
    q_ref[32:34] = tail[...].reshape(2, 16, 128).astype(BF)
    for place in range(32):
        q_ref[place] = in_ref[place, 0:16, :]
        for there in range(4):
            kv_ref[there, place] = in_ref[place, 16:48, :]


def spread(at, lists, mine):
    vmem = pl.BlockSpec(memory_space=pltpu.VMEM)
    return pl.pallas_call(
        spread_kernel,
        out_shape=[
            jax.ShapeDtypeStruct((34, 16, 128), BF),
            jax.ShapeDtypeStruct((4, 32, 32, 128), BF),
        ],
        in_specs=[pl.BlockSpec(memory_space=pltpu.SMEM)] + [vmem] * 5,
        out_specs=[vmem, vmem],
        scratch_shapes=[pltpu.VMEM((4, 8, 128), F32)],
        compiler_params=small,
        name="spread",
    )(at, *lists, mine)


def attend_kernel(
    at_ref, q0, q1, q2, q3, kv_in, out_ref,
    q_ref, kv_ref, vt_ref, qt_ref, sums_ref, acc_ref, rows_ref, list_ref, sems,

):
    x, core = at_ref[0], at_ref[4]
    to_q = [pltpu.make_async_copy(q, q_ref.at[d], sems.at[d]) for d, q in enumerate((q0, q1, q2, q3))]
    to_kv = [pltpu.make_async_copy(kv_in.at[d], kv_ref.at[d], sems.at[4 + d]) for d in range(4)]
    for copy in to_q + to_kv:
        copy.start()
    scale = LOG2E / 128**0.5
    for dq in range(4):
        to_q[dq].wait()
        rows_ref[dq] = q_ref[dq, 32:34].reshape(32, 128).astype(F32).astype(jnp.int32)
    to_scalars = pltpu.make_async_copy(rows_ref, list_ref, sems.at[8])
    to_scalars.start()
    for dq in range(4):
        for zq in range(4):
            qt_ref[dq * 4 + zq] = q_ref[dq, zq * 8 : zq * 8 + 8].reshape(128, 128).T
    for yk in range(4):
        to_kv[yk].wait()
        for zk in range(4):
            value = kv_ref[yk, zk * 8 : zk * 8 + 8, 16:32, :].reshape(128, 128)
            vt_ref[yk * 4 + zk] = value.T
    to_scalars.wait()

    counts = [list_ref[at // 4, at % 4 * 8 + x, 16] for at in range(16)]

    def look(at, step, state):
        keys, turned, biases = [], [], []
        for part in range(4):
            place = step * 4 + part
            here = place < counts[at]
            block = jnp.where(here, list_ref[at // 4, at % 4 * 8 + x, jnp.where(here, place, 0)], 0)
            cut = pl.ds(pl.multiple_of((block % 4) * 8, 8), 8)
            keys.append(kv_ref[block // 4, cut, 0:16, :].reshape(128, 128))
            turned.append(vt_ref[block])
            biases.append(jnp.where(here, 0.0, LOW))
        raw = jnp.dot(jnp.concatenate(keys, axis=0), qt_ref[at], preferred_element_type=F32)
        scores = jnp.concatenate(
            [raw[i * 128 : i * 128 + 128] * scale + biases[i] for i in range(4)], axis=0
        )
        new = jnp.max(scores, axis=0, keepdims=True)
        if state is not None:
            new = jnp.maximum(state[0], new)
        weights = jnp.exp2(scores - new)
        total = jnp.sum(weights, axis=0, keepdims=True)
        acc = jnp.dot(
            jnp.concatenate(turned, axis=1), weights.astype(BF), preferred_element_type=F32
        )
        if state is not None:
            again = jnp.exp2(state[0] - new)
            total = state[1] * again + total
            acc = state[2] * again + acc
        return new, total, acc

    def keep(at, state):
        sums_ref[at, 0:1, :] = state[0]
        sums_ref[at, 1:2, :] = state[1]
        acc_ref[at] = state[2]

    def kept(at):
        return sums_ref[at, 0:1, :], sums_ref[at, 1:2, :], acc_ref[at]

    for at in range(16):
        keep(at, look(at, 0, None))

    for group in range(4):
        ats = range(group * 4, group * 4 + 4)
        most = counts[ats[0]]
        for at in ats[1:]:
            most = jnp.maximum(most, counts[at])

        @pl.loop(1, (most + 3) // 4)
        def _(step, ats=ats):
            for at in ats:
                keep(at, look(at, step, kept(at)))

    for at in range(16):
        largest, total, acc = kept(at)
        xq, zq = (x + jnp.where(core == 0, 4 - at // 4, at // 4)) % 4, at % 4
        o = (acc * (1.0 / total)).T.astype(BF)
        lse = jnp.where(counts[at] > 0, largest + jnp.log2(total), LOW)
        hi = lse.astype(BF)
        rest = lse - hi.astype(F32)
        mid = rest.astype(BF)
        lo = (rest - mid.astype(F32)).astype(BF)
        coded = jnp.concatenate(
            [hi.astype(F32), mid.astype(F32), lo.astype(F32), jnp.zeros((5, 128), F32)], axis=0
        )
        other = jnp.concatenate([coded[:, 64:], coded[:, :64]], axis=1)
        out_ref[xq, zq * 2, 0:64, :] = o[0:64]
        out_ref[xq, zq * 2, 64:72, :] = coded.astype(BF)
        out_ref[xq, zq * 2 + 1, 0:64, :] = o[64:128]
        out_ref[xq, zq * 2 + 1, 64:72, :] = other.astype(BF)


def attend(at, qs, kv):
    smem = pl.BlockSpec(memory_space=pltpu.SMEM)
    vmem = pl.BlockSpec(memory_space=pltpu.VMEM)
    return pl.pallas_call(
        attend_kernel,
        out_shape=jax.ShapeDtypeStruct((4, 8, ROWS, 128), BF),
        in_specs=[smem] + [pl.BlockSpec(memory_space=pl.ANY)] * 5,
        out_specs=vmem,
        scratch_shapes=[
            pltpu.VMEM((4, 34, 16, 128), BF),
            pltpu.VMEM((4, 32, 32, 128), BF),
            pltpu.VMEM((16, 128, 128), BF),
            pltpu.VMEM((16, 128, 128), BF),
            pltpu.VMEM((16, 8, 128), F32),
            pltpu.VMEM((16, 128, 128), F32),
            pltpu.VMEM((4, 32, 128), jnp.int32),
            pltpu.SMEM((4, 32, 128), jnp.int32),
            pltpu.SemaphoreType.DMA((9,)),
        ],
        compiler_params=pltpu.CompilerParams(vmem_limit_bytes=44 * 1024 * 1024),
        cost_estimate=pl.CostEstimate(flops=1 << 30, bytes_accessed=2 << 20, transcendentals=1 << 21),
        name="attend",
    )(at, *qs, kv)


def project_kernel(at_ref, parts_ref, own_ref, other_in, y0, y1, y2, y3, att_ref, other_ref, sems):
    arriving = []
    for cut in range(6):
        columns = slice(cut * 512, cut * 512 + 512)
        arriving.append(
            pltpu.make_async_copy(other_in.at[:, columns], other_ref.at[:, columns], sems.at[cut])
        )
        arriving[-1].start()
    z_hi, core = at_ref[3], at_ref[4]
    coded = [parts_ref[i // 8, i % 8, 64:72, :].astype(F32) for i in range(32)]
    lse = jnp.concatenate([c[0:1] + c[1:2] + c[2:3] for c in coded], axis=0)
    groups = [lse[8 * i : 8 * i + 8] for i in range(4)]
    top = jnp.maximum(jnp.maximum(groups[0], groups[1]), jnp.maximum(groups[2], groups[3]))
    shares = [jnp.exp2(g - top) for g in groups]
    inverse = 1.0 / (shares[0] + shares[1] + shares[2] + shares[3])
    share = jnp.concatenate([s * inverse for s in shares], axis=0)
    share = jnp.concatenate([share, jnp.zeros((96, 128), F32)], axis=0).T
    for slot in range(3):
        for there in range(2):
            summed = None
            for xk in range(4):
                i = slot * 2 + there
                term = parts_ref[xk, i, 0:64, :].astype(F32) * share[0:64, xk * 8 + i : xk * 8 + i + 1]
                summed = term if summed is None else summed + term
            att_ref[there, :, slot * 128 : slot * 128 + 128] = summed.astype(BF)

    rows = []
    for d in range(4):
        there = (z_hi + jnp.where(core == 0, d, 4 - d)) % 4
        rows.append(pl.ds(pl.multiple_of(there * 16, 16), 16))
    own = jnp.concatenate([att_ref[core, r, :] for r in rows], axis=0)
    other = jnp.concatenate([att_ref[1 - core, r, :] for r in rows], axis=0)
    for cut in range(0, 3072, 512):
        columns = slice(cut, cut + 512)
        y = jnp.dot(own, own_ref[:, columns], preferred_element_type=F32)
        arriving[cut // 512].wait()
        y = (y + jnp.dot(other, other_ref[:, columns], preferred_element_type=F32)).astype(BF)
        for d, y_ref in enumerate((y0, y1, y2, y3)):
            y_ref[:, columns] = y[d * 16 : d * 16 + 16]


def project(at, parts, own, other):
    vmem = pl.BlockSpec(memory_space=pltpu.VMEM)
    return pl.pallas_call(
        project_kernel,
        out_shape=[jax.ShapeDtypeStruct((16, 3072), BF)] * 4,
        in_specs=[
            pl.BlockSpec(memory_space=pltpu.SMEM),
            vmem,
            vmem,
            pl.BlockSpec(memory_space=pl.ANY),
        ],
        out_specs=[vmem] * 4,
        scratch_shapes=[
            pltpu.VMEM((2, 64, 384), BF),
            pltpu.VMEM((384, 3072), BF),
            pltpu.SemaphoreType.DMA((6,)),
        ],
        compiler_params=small,
        name="project",
    )(at, parts, own, other)


def turn(array, axis, step):
    return lax.ppermute(array, axis, [(i, (i + step) % 4) for i in range(4)])


def turn_apart(array, axis, step):
    names = (axis, "core") if axis == "z_hi" else ("core", axis)
    pairs = []
    for core in range(2):
        for i in range(4):
            j = (i + (step if core == 0 else -step)) % 4
            pairs.append((2 * i + core, 2 * j + core) if axis == "z_hi" else (4 * core + i, 4 * core + j))
    return lax.ppermute(array, names, pairs)


def local(queries, keys_in, values, block_mask, w_out):
    x, y, z = lax.axis_index("x"), lax.axis_index("y"), lax.axis_index("z_lo")
    z_hi, core = lax.axis_index("z_hi"), lax.axis_index("core")
    at = jnp.stack([x, y, jnp.minimum(z, 2), z_hi, core, z]).astype(jnp.int32)
    chosen = choose(block_mask)
    lists = [chosen] + [turn(chosen, "z_lo", d) for d in (1, 2, 3)]
    packed = pack(queries, keys_in, values)
    mine = lax.all_to_all(packed, ("z_lo", "core", "z_hi"), split_axis=0, concat_axis=0, tiled=True)
    q, kv = spread(at, lists, mine)
    q, w_here = lax.optimization_barrier((q, w_out))
    w_other = lax.ppermute(w_here, "core", [(0, 1), (1, 0)])
    qs = [q] + [turn_apart(q, "x", d) for d in (1, 2, 3)]
    kv = lax.all_to_all(kv, "y", split_axis=0, concat_axis=0, tiled=True)
    parts = attend(at, qs, kv)
    parts = lax.all_to_all(
        parts.reshape(32, ROWS, 128), ("x", "z_lo", "core"), split_axis=0, concat_axis=0, tiled=True
    )
    ys = project(at, parts.reshape(4, 8, ROWS, 128), w_out, w_other)
    far, right, left = [turn_apart(ys[d], "z_hi", d).astype(F32) for d in (2, 1, 3)]
    return (((ys[0].astype(F32) + far) + right) + left).astype(BF)


def solution(mesh):
    fine = Mesh(mesh.devices.reshape(4, 2, 4, 4, 4), AXES)
    tokens = P(("z_lo", "x", "y", "z_hi", "core"), None)
    placed = (
        tokens,
        tokens,
        tokens,
        P(("z_hi", "core"), ("z_lo", "x", "y"), None),
        P(("z_hi", "core"), None),
    )
    return jax.shard_map(local, mesh=fine, in_specs=placed, out_specs=tokens, check_vma=False)
```
